128 devices in a mesh: dp: 16 (over x, y_hi, core), tensor: 8 (over z, y_lo).
Axes of the slice: x: 4, y: 4 (y_hi: 2, y_lo: 2; y = y_hi * 2 + y_lo), z: 4, core: 2. Of those that a mesh axis runs over, the one named last changes fastest.
Arguments:
- context: bfloat16 [16384, 6144], P('dp', 'tensor'), may hold values from -6 to 6
- cotangent: bfloat16 [16384, 6144], P(('dp', 'tensor')), may hold values from -24 to 24
- weight: bfloat16 [6144, 6144], P(None, 'tensor'), may hold values from -49 to 49
- first_moment: float32 [6144, 6144], P('dp', 'tensor'), may hold values from -49 to 49
- second_moment: float32 [6144, 6144], P('dp', 'tensor'), may hold values from 0.25 to 4
Outputs:
- context_grad: bfloat16 [16384, 6144], P('dp', 'tensor')
- momentum: float32 [6144, 6144], P('dp', 'tensor')
- variance: float32 [6144, 6144], P('dp', 'tensor')
- lamb_step: float32 [6144, 6144], P('dp', 'tensor')
The draws below stay inside these ranges and needn't reach their ends.
All inputs are finite; a program needn't handle non-finite values.
Results may differ from the reference program's by a relative error of at most 0.0065.
Values may be sent and summed in bfloat16 or wider, within the bound.
A program may use at most 192 MiB of HBM per device.

```python
import math
import jax
import jax.numpy as jnp

D = 6144
HEADS = 48
HD = 128
INNER = 6144
TOKENS = 16384


def scale_profile(key, row_count, col_count, ceiling):
    row_key, col_key = jax.random.split(key)
    row_power = jax.random.uniform(row_key, (row_count, 1), jnp.float32)
    col_power = jax.random.uniform(col_key, (1, col_count), jnp.float32)
    row_rise = 1.0 + 0.75 * jnp.arange(row_count, dtype=jnp.float32)[:, None] / row_count
    col_rise = 1.0 + 0.75 * jnp.arange(col_count, dtype=jnp.float32)[None, :] / col_count
    spread = (ceiling * ceiling - 1.0) / (2.0 * math.log(ceiling))
    return jnp.sqrt(row_rise * col_rise) * jnp.exp((row_power + col_power) * math.log(ceiling)) / spread


def scaled_values(key):
    value_key, scale_key = jax.random.split(key)
    values = jnp.clip(jax.random.normal(value_key, (D, INNER), jnp.float32), -6.0, 6.0)
    ceiling = 10.0
    return values * scale_profile(scale_key, D, INNER, ceiling)


def draw_weight(key, part):
    key = jax.random.fold_in(key, 11)
    return scaled_values(key).astype(jnp.bfloat16)


def draw_first_moment(key, part):
    key = jax.random.fold_in(key, 23)
    return scaled_values(key).astype(jnp.float32)


def strengthened(entries, stream_key, source, target, parts, factor):
    def block_of(dim):
        return (jnp.arange(entries.shape[dim]) // (entries.shape[dim] // parts)).reshape((-1,) + (1,) * (entries.ndim - 1 - dim))

    first = jax.random.permutation(stream_key, parts)[block_of(target)]
    far = (block_of(target) + parts // 2) % parts
    return jnp.where((block_of(source) == first) | (block_of(source) == far), factor * entries, entries)


def steps_of(rng, shape, pieces, least, largest):
    factor_of, own = 1.0, jax.random.fold_in(rng, 6)
    for dim, shards_of in pieces:
        steps = jnp.exp(jax.random.uniform(jax.random.fold_in(own, dim), (shards_of,), jnp.float32, least / len(pieces), largest / len(pieces)))
        factor_of = factor_of * jnp.repeat(steps, shape[dim] // shards_of).reshape([-1 if axis == dim else 1 for axis in range(len(shape))])
    return factor_of


def scatter_about(rng, shape, deviation, bound, shards=(), kind=jnp.bfloat16):
    level = steps_of(rng, shape, shards, -0.22, 0.18) if shards else 1.0
    array = jax.random.normal(rng, shape, jnp.float32) * deviation * level
    return jnp.minimum(jnp.maximum(array, -bound), bound).astype(kind)


def heavy_noise(key, extent, scale, bound, shards, heavy, kind=jnp.bfloat16):
    array = scale * jax.random.normal(key, extent, jnp.float32)
    if shards:
        array = array * steps_of(key, extent, shards, -0.22, 0.18)
    return jnp.clip(strengthened(array, jax.random.fold_in(key, 3), *heavy), -bound, bound).astype(kind)


def setup_inputs(seed: int = 0) -> dict:
    splits = jax.random.split(jax.random.key(seed), 6)
    return {
        "context": scatter_about(splits[0], (TOKENS, INNER), 1.0, 6.0, ((0, 16), (1, 8))),
        "cotangent": heavy_noise(splits[1], (TOKENS, D), 1.0, 24.0, ((0, 128),), (0, 1, 128, 5.5)),
        "weight": draw_weight(jax.random.fold_in(splits[5], 71), 0),
        "first_moment": draw_first_moment(jax.random.fold_in(splits[5], 71), 0),
        "second_moment": jnp.clip(jnp.exp(math.log(4.0) - 2.7725887 * jax.random.uniform(splits[4], (D, INNER), jnp.float32) ** steps_of(splits[4], (D, INNER), ((0, 16), (1, 8)), -0.2, 0.2)), 0.25, 4.0),
    }


def reference(context, cotangent, weight, first_moment, second_moment):
    multiplier = 1.0 / math.sqrt(HEADS * HD)
    context_grad = (jnp.dot(cotangent, weight, preferred_element_type=jnp.float32) * multiplier).astype(jnp.bfloat16)
    grad = jnp.dot(cotangent.T, context, preferred_element_type=jnp.float32) * multiplier
    momentum = 0.9 * first_moment + 0.1 * grad
    variance = 0.95 * second_moment + 0.05 * grad * grad
    weight_full = weight.astype(jnp.float32)
    update = momentum / (jnp.sqrt(variance) + 1e-06) + 0.1 * weight_full
    weight_sq = jnp.sum(weight_full * weight_full)
    update_sq = jnp.sum(update * update)
    lamb_step = jnp.sqrt(weight_sq) / jnp.sqrt(update_sq + 1e-06) * update
    return (context_grad, momentum, variance, lamb_step)
```

```python
import functools
import math

import jax
import jax.numpy as jnp
from jax import lax
from jax.experimental import pallas as pl
from jax.experimental.pallas import tpu as pltpu
from jax.sharding import PartitionSpec as P

HEADS = 48
HD = 128
MESH = pl.DeviceIdType.MESH
PARTS = 8
F32 = jnp.float32
BF16 = jnp.bfloat16

MESSAGES = (
    ("z+", 0, 0, 0, 128),
    ("z-", 0, 0, 0, 128),
    ("y", 0, 0, 0, 128),
    ("z+", 0, 1, 0, 80),
    ("z-", 0, 1, 0, 80),
    ("z+", 3, 0, 0, 64),
    ("z-", 1, 0, 64, 128),
    ("y", 3, 0, 80, 128),
    ("y", 1, 0, 80, 128),
    ("z+", 3, 1, 0, 48),
    ("z-", 1, 1, 48, 80),
    ("y", 2, 0, 80, 128),
)


def kernel(
    multiplier,
    cot, ctx, weight, first, second,
    cg_out, mo_out, va_out, la_out,
    gath, wv, cx, cxt, prod, cr, xr, ys, yr, acc, cgb, mb, vb, up, base, one, two,
    own_sem, w_sem, in_sem, out_sem, gs, gr, ds_, dr, xs_, xr_, ysem, s1, r1, s2, r2,
):
    d, t = lax.axis_index("dp"), lax.axis_index("tensor")
    x, yh, c = d // 4, (d // 2) % 2, d % 2
    z, yl = t // 2, t % 2
    half = gath.shape[2] // 2
    rows = cot.shape[0]

    def device(x, yh, c, z, yl):
        return ((x * 2 + yh) * 2 + c, z * 2 + yl)

    links = {
        "z+": device(x, yh, c, (z + 1) % 4, yl),
        "z-": device(x, yh, c, (z + 3) % 4, yl),
        "y": device(x, yh, c, z, 1 - yl),
    }
    sibling = device(x, yh, 1 - c, z, yl)

    def offset(s, h):
        r = s % 4
        return ((2 + 3 * r + 3 * (r * (r - 1) // 2)) * (1 + 2 * h)) % 4

    def owner(s, h):
        oy = (yh + 1 - s // 4) % 2
        return (((x + offset(s, h)) % 4) * 2 + oy) * 2 + h

    def own_copy(s, h):
        at = pl.multiple_of(owner(s, h) * half, 128)
        return pltpu.make_async_copy(
            cot.at[:, pl.ds(at, half)],
            gath.at[s, pl.ds(pl.multiple_of(t * rows, rows), rows), pl.ds(h * half, half)],
            own_sem.at[s, h],
        )

    def w_copy(s, h):
        at = pl.multiple_of(owner(s, h) * half, 128)
        return pltpu.make_async_copy(
            weight.at[pl.ds(at, half)], wv.at[s, pl.ds(h * half, half)], w_sem.at[s, h]
        )

    ctx_copy = pltpu.make_async_copy(ctx, cx, in_sem.at[0])
    first_copy = pltpu.make_async_copy(first, mb, in_sem.at[1])
    second_copy = pltpu.make_async_copy(second, vb, in_sem.at[2])

    def message(s, k, received):
        link, dz, yb, lo, hi = MESSAGES[k]
        if received:
            dz = (dz + {"z+": 3, "z-": 1, "y": 0}[link]) % 4
            yb = 1 - yb if link == "y" else yb
        block = ((z + dz) % 4) * 2 + (1 - yl if yb else yl)
        ref = gath.at[s, pl.ds(pl.multiple_of(block * rows + lo, 16), hi - lo)]
        return pltpu.make_async_remote_copy(
            src_ref=ref, dst_ref=ref, send_sem=gs.at[s, k], recv_sem=gr.at[s, k],
            device_id=links[link], device_id_type=MESH,
        )

    def send(s, *ks):
        for k in ks:
            message(s, k, False).start()

    def arrive(s, *ks):
        for k in ks:
            message(s, k, True).wait_recv()

    def stage_a(s):
        for h in range(2):
            own_copy(s, h).wait()
        send(s, 0, 1, 2)

    def stage_b(s):
        arrive(s, 2)
        send(s, 3, 4)
        arrive(s, 0)
        send(s, 5, 7)
        arrive(s, 1)
        send(s, 6, 8)

    def stage_c(s):
        arrive(s, 3)
        send(s, 9)
        arrive(s, 4)
        send(s, 10)
        arrive(s, 6)
        send(s, 11)

    def core_copy(s):
        return pltpu.make_async_remote_copy(
            src_ref=prod.at[s, 1 - c], dst_ref=cr.at[s], send_sem=ds_.at[s], recv_sem=dr.at[s],
            device_id=sibling, device_id_type=MESH,
        )

    def x_copy(s):
        dx = offset(s, c)
        slot = (1 - s // 4) * 3 + (dx + 3) % 4
        return pltpu.make_async_remote_copy(
            src_ref=prod.at[s, c], dst_ref=xr.at[slot], send_sem=xs_.at[s], recv_sem=xr_.at[slot],
            device_id=device((x + dx) % 4, yh, c, z, yl), device_id_type=MESH,
        )

    def x_arrive(slot):
        pltpu.make_async_remote_copy(
            src_ref=xr.at[slot], dst_ref=xr.at[slot], send_sem=xs_.at[0], recv_sem=xr_.at[slot],
            device_id=sibling, device_id_type=MESH,
        ).wait_recv()

    y_copy = pltpu.make_async_remote_copy(
        src_ref=ys, dst_ref=yr, send_sem=ysem.at[0], recv_sem=ysem.at[1],
        device_id=device(x, 1 - yh, c, z, yl), device_id_type=MESH,
    )

    group1 = [
        ((x + dx) % 4, (c + dc) % 2, (dx * 2 + dc)) for dx in range(4) for dc in range(2) if dx or dc
    ]
    y = yh * 2 + yl
    group2 = [
        ((y + dy) % 4, (z + dz) % 4, (dy * 4 + dz)) for dy in range(4) for dz in range(4) if dy or dz
    ]

    def one_copy(px, pc, slot):
        return pltpu.make_async_remote_copy(
            src_ref=one.at[0], dst_ref=one.at[slot], send_sem=s1.at[slot], recv_sem=r1.at[slot],
            device_id=device(px, yh, pc, z, yl), device_id_type=MESH,
        )

    def two_copy(py, pz, slot):
        return pltpu.make_async_remote_copy(
            src_ref=two.at[0], dst_ref=two.at[slot], send_sem=s2.at[slot], recv_sem=r2.at[slot],
            device_id=device(x, py // 2, c, pz, py % 2), device_id_type=MESH,
        )

    for s in range(PARTS):
        for h in range(2):
            own_copy(s, h).start()
        if s == 0:
            ctx_copy.start()
    for s in range(PARTS):
        for h in range(2):
            w_copy(s, h).start()
    first_copy.start()
    second_copy.start()

    barrier = pltpu.get_barrier_semaphore()
    for px, pc, _ in group1:
        pl.semaphore_signal(barrier, inc=1, device_id=device(px, yh, pc, z, yl), device_id_type=MESH)
    for py, pz, _ in group2:
        pl.semaphore_signal(barrier, inc=1, device_id=device(x, py // 2, c, pz, py % 2), device_id_type=MESH)
    pl.semaphore_wait(barrier, len(group1) + len(group2))

    stage_a(0)
    ctx_copy.wait()
    for k in range(cx.shape[0] // 128):
        cxt[:, k * 128 : (k + 1) * 128] = cx[k * 128 : (k + 1) * 128, :].T

    def product(s):
        for n in range(2 * half // 256):
            value = jnp.dot(cxt[...], gath[s, :, n * 256 : (n + 1) * 256], preferred_element_type=F32)
            value = (value * multiplier).astype(BF16)
            for k in range(2):
                column = n * 256 + k * 128
                prod[s, column // half, :, column % half : column % half + 128] = value[:, k * 128 : (k + 1) * 128]

    def context_part(s, last):
        for h in range(2):
            w_copy(s, h).wait()

        @pl.loop(0, acc.shape[1] // 256)
        def _(n):
            cols = pl.ds(pl.multiple_of(n * 256, 256), 256)
            value = jnp.dot(gath[s], wv[s, :, cols], preferred_element_type=F32)
            if last:
                cgb[:, cols] = ((acc[:, cols] + value) * multiplier).astype(BF16)
            else:
                acc[:, cols] += value

    def whole(s):
        arrive(s, 5, 7, 8, 9, 10, 11)
        product(s)
        core_copy(s).start()

    acc[...] = jnp.zeros_like(acc)

    @pl.loop(0, PARTS + 1)
    def _(i):
        @pl.when(i < PARTS - 1)
        def _():
            stage_a(i + 1)

        @pl.when(i < PARTS)
        def _():
            stage_b(i)

        @pl.when(i > 0)
        def _():
            stage_c(i - 1)

        @pl.when(i > 1)
        def _():
            s = i - 2
            whole(s)
            context_part(s, False)
            core_copy(s).wait_recv()

            @pl.when(s % 4 != 3)
            def _():
                prod[s, c] = (prod[s, c].astype(F32) + cr[s].astype(F32)).astype(BF16)
                x_copy(s).start()

            @pl.when(s == 3)
            def _():
                for slot in range(3, 6):
                    x_arrive(slot)
                total = prod[s, c].astype(F32) + cr[s].astype(F32)
                for slot in range(3, 6):
                    total += xr[slot].astype(F32)
                ys[...] = total.astype(BF16)
                y_copy.start()

    s = PARTS - 1
    whole(s)
    y_copy.wait_recv()
    base[...] = yr[...].astype(F32)
    for slot in range(3):
        x_arrive(slot)
        base[...] += xr[slot].astype(F32)
    context_part(s, True)
    cg_copy = pltpu.make_async_copy(cgb, cg_out, out_sem.at[0])
    cg_copy.start()
    first_copy.wait()
    second_copy.wait()
    core_copy(s).wait_recv()

    def fold(value):
        total = value[0:8, 0:128]
        for r in range(value.shape[0] // 8):
            for k in range(value.shape[1] // 128):
                if r or k:
                    total += value[r * 8 : (r + 1) * 8, k * 128 : (k + 1) * 128]
        return total

    zero = jnp.zeros((8, 128), F32)
    u_sum, w_sum = zero, zero
    for k in range(half // 128):
        cols = slice(k * 128, (k + 1) * 128)
        g = (base[:, cols] + prod[s, c, :, cols].astype(F32) + cr[s, :, cols].astype(F32)).T
        w = wv[s, pl.ds(pl.multiple_of(c * half + k * 128, 128), 128), :].astype(F32)
        m = 0.9 * mb[cols, :] + 0.1 * g
        v = 0.95 * vb[cols, :] + 0.05 * g * g
        u = m / (jnp.sqrt(v) + 1e-06) + 0.1 * w
        mb[cols, :] = m
        vb[cols, :] = v
        up[cols, :] = u
        u_sum += fold(u * u)
        w_sum += fold(w * w)
    one[0, 0:8] = u_sum
    one[0, 8:16] = w_sum
    for px, pc, slot in group1:
        one_copy(px, pc, slot).start()
    mo_copy = pltpu.make_async_copy(mb, mo_out, out_sem.at[1])
    va_copy = pltpu.make_async_copy(vb, va_out, out_sem.at[2])
    mo_copy.start()
    va_copy.start()
    for px, pc, slot in group1:
        one_copy(px, pc, slot).wait_recv()
    total = one[0]
    for _, _, slot in group1:
        total += one[slot]
    two[0] = total
    for py, pz, slot in group2:
        two_copy(py, pz, slot).start()
    for py, pz, slot in group2:
        two_copy(py, pz, slot).wait_recv()
    total = two[0]
    for _, _, slot in group2:
        total += two[slot]
    u_total = jnp.sum(total[0:8], keepdims=True)
    w_total = jnp.sum(total[8:16], keepdims=True)
    up[...] = up[...] * (jnp.sqrt(w_total) / jnp.sqrt(u_total + 1e-06))
    la_copy = pltpu.make_async_copy(up, la_out, out_sem.at[3])
    la_copy.start()

    @pl.loop(0, PARTS)
    def _(s):
        for k in range(len(MESSAGES)):
            message(s, k, False).wait_send()
        core_copy(s).wait_send()

        @pl.when(s % 4 != 3)
        def _():
            x_copy(s).wait_send()

    y_copy.wait_send()
    for px, pc, slot in group1:
        one_copy(px, pc, slot).wait_send()
    for py, pz, slot in group2:
        two_copy(py, pz, slot).wait_send()
    cg_copy.wait()
    mo_copy.wait()
    va_copy.wait()
    la_copy.wait()


def shards(context, cotangent, weight, first_moment, second_moment):
    multiplier = 1.0 / math.sqrt(HEADS * HD)
    tokens, inner = context.shape
    rows, model = cotangent.shape
    part = model // PARTS
    half = part // 2
    sem = pltpu.SemaphoreType.DMA
    n = len(MESSAGES)
    scratch = [
        pltpu.VMEM((PARTS, tokens, part), BF16),
        pltpu.VMEM((PARTS, part, inner), BF16),
        pltpu.VMEM((tokens, inner), BF16),
        pltpu.VMEM((inner, tokens), BF16),
        pltpu.VMEM((PARTS, 2, inner, half), BF16),
        pltpu.VMEM((PARTS, inner, half), BF16),
        pltpu.VMEM((6, inner, half), BF16),
        pltpu.VMEM((inner, half), BF16),
        pltpu.VMEM((inner, half), BF16),
        pltpu.VMEM((tokens, inner), F32),
        pltpu.VMEM((tokens, inner), BF16),
        pltpu.VMEM((half, inner), F32),
        pltpu.VMEM((half, inner), F32),
        pltpu.VMEM((half, inner), F32),
        pltpu.VMEM((inner, half), F32),
        pltpu.VMEM((8, 16, 128), F32),
        pltpu.VMEM((16, 16, 128), F32),
        sem((PARTS, 2)),
        sem((PARTS, 2)),
        sem((3,)),
        sem((4,)),
        sem((PARTS, n)),
        sem((PARTS, n)),
        sem((PARTS,)),
        sem((PARTS,)),
        sem((PARTS,)),
        sem((6,)),
        sem((2,)),
        sem((8,)),
        sem((8,)),
        sem((16,)),
        sem((16,)),
    ]
    state = jax.ShapeDtypeStruct(first_moment.shape, F32)
    return pl.pallas_call(
        functools.partial(kernel, multiplier),
        out_shape=(jax.ShapeDtypeStruct(context.shape, BF16), state, state, state),
        in_specs=[pl.BlockSpec(memory_space=pl.ANY)] * 5,
        out_specs=[pl.BlockSpec(memory_space=pl.ANY)] * 4,
        scratch_shapes=scratch,
        compiler_params=pltpu.CompilerParams(
            collective_id=0, has_side_effects=True, vmem_limit_bytes=63 * 2**20
        ),
        cost_estimate=pl.CostEstimate(
            flops=4 * tokens * inner * model, bytes_accessed=40 * 2**20, transcendentals=0
        ),
        name="step",
    )(cotangent, context, weight, first_moment, second_moment)


def solution(mesh):
    in_specs = (
        P("dp", "tensor"),
        P(("dp", "tensor"), None),
        P(None, "tensor"),
        P("dp", "tensor"),
        P("dp", "tensor"),
    )
    out_specs = (P("dp", "tensor"), P("dp", "tensor"), P("dp", "tensor"), P("dp", "tensor"))
    return jax.shard_map(shards, mesh=mesh, in_specs=in_specs, out_specs=out_specs, check_vma=False)
```

```python
import functools
import math

import jax
import jax.numpy as jnp
from jax import lax
from jax.experimental import pallas as pl
from jax.experimental.pallas import tpu as pltpu
from jax.sharding import PartitionSpec as P

HEADS = 48
HD = 128
MESH = pl.DeviceIdType.MESH
PARTS = 8
F32 = jnp.float32
BF16 = jnp.bfloat16

MESSAGES = (
    ("z+", 0, 0, 0, 128),
    ("z-", 0, 0, 0, 128),
    ("y", 0, 0, 0, 128),
    ("z+", 0, 1, 0, 80),
    ("z-", 0, 1, 0, 80),
    ("z+", 3, 0, 0, 64),
    ("z-", 1, 0, 64, 128),
    ("y", 3, 0, 80, 128),
    ("y", 1, 0, 80, 128),
    ("z+", 3, 1, 0, 48),
    ("z-", 1, 1, 48, 80),
    ("y", 2, 0, 80, 128),
    ("z+", 3, 1, 0, 32),
    ("z-", 1, 1, 32, 80),
)
SLOTS = 12


def kernel(
    multiplier,
    cot, ctx, weight, first, second,
    cg, mo, va, up, sums,
    gath, wv, cx, cxt, prod, cr, xr, ys, yr, acc, base, one, two,
    own_sem, w_sem, in_sem, gs, gr, gs7, gr7, ds_, dr, xs_, xr_, ysem, s1, r1, s2, r2,
):
    d, t = lax.axis_index("dp"), lax.axis_index("tensor")
    x, yh, c = d // 4, (d // 2) % 2, d % 2
    z, yl = t // 2, t % 2
    half = gath.shape[2] // 2
    rows = cot.shape[0]
    last = PARTS - 1

    def device(x, yh, c, z, yl):
        return ((x * 2 + yh) * 2 + c, z * 2 + yl)

    links = {
        "z+": device(x, yh, c, (z + 1) % 4, yl),
        "z-": device(x, yh, c, (z + 3) % 4, yl),
        "y": device(x, yh, c, z, 1 - yl),
    }
    sibling = device(x, yh, 1 - c, z, yl)

    def offset(s, h):
        r = s % 4
        return ((2 + 3 * r + 3 * (r * (r - 1) // 2)) * (1 + 2 * h)) % 4

    def owner(s, h):
        oy = (yh + 1 - s // 4) % 2
        h = (h + (1 - c) * (s // last)) % 2
        return (((x + offset(s, h)) % 4) * 2 + oy) * 2 + h

    def own_copy(s, h):
        at = pl.multiple_of(owner(s, h) * half, 128)
        return pltpu.make_async_copy(
            cot.at[:, pl.ds(at, half)],
            gath.at[s, pl.ds(pl.multiple_of(t * rows, rows), rows), pl.ds(h * half, half)],
            own_sem.at[s, h],
        )

    def w_copy(s, h):
        at = pl.multiple_of(owner(s, h) * half, 128)
        return pltpu.make_async_copy(
            weight.at[pl.ds(at, half)], wv.at[s, pl.ds(h * half, half)], w_sem.at[s, h]
        )

    ctx_copy = pltpu.make_async_copy(ctx, cx, in_sem.at[0])
    first_copy = pltpu.make_async_copy(first, mo, in_sem.at[1])
    second_copy = pltpu.make_async_copy(second, va, in_sem.at[2])

    def message(s, k, received, part=None):
        link, dz, yb, lo, hi = MESSAGES[k]
        if received:
            dz = (dz + {"z+": 3, "z-": 1, "y": 0}[link]) % 4
            yb = 1 - yb if link == "y" else yb
        block = ((z + dz) % 4) * 2 + (1 - yl if yb else yl)
        at = pl.ds(pl.multiple_of(block * rows + lo, 16), hi - lo)
        slot = k if k < SLOTS else k - SLOTS + 9
        if part is None:
            ref, sent, got = gath.at[s, at], gs.at[s, slot], gr.at[s, slot]
        else:
            ref = gath.at[s, at, pl.ds(part * half, half)]
            sent, got = gs7.at[part, slot], gr7.at[part, slot]
        return pltpu.make_async_remote_copy(
            src_ref=ref, dst_ref=ref, send_sem=sent, recv_sem=got,
            device_id=links[link], device_id_type=MESH,
        )

    def send(s, *ks, part=None):
        for k in ks:
            message(s, k, False, part).start()

    def arrive(s, *ks, part=None):
        for k in ks:
            message(s, k, True, part).wait_recv()

    def by_parity(s, action):
        @pl.when(s % 2 == 0)
        def _():
            for k in (9, 10):
                action(k)

        @pl.when(s % 2 == 1)
        def _():
            for k in (12, 13):
                action(k)

    def stage_a(s):
        for h in range(2):
            own_copy(s, h).wait()
        send(s, 0, 1, 2)

    def stage_b(s):
        arrive(s, 2)
        send(s, 3, 4)
        arrive(s, 0)
        send(s, 5, 7)
        arrive(s, 1)
        send(s, 6, 8)

    def stage_c(s):
        arrive(s, 3)
        arrive(s, 4)
        by_parity(s, lambda k: send(s, k))
        arrive(s, 6)
        send(s, 11)

    def core_copy(s, part=None):
        src = prod.at[s, 1 - c] if part is None else prod.at[s, part]
        return pltpu.make_async_remote_copy(
            src_ref=src, dst_ref=cr.at[s], send_sem=ds_.at[s], recv_sem=dr.at[s],
            device_id=sibling, device_id_type=MESH,
        )

    def x_copy(s):
        dx = offset(s, c)
        slot = (1 - s // 4) * 3 + (dx + 3) % 4
        return pltpu.make_async_remote_copy(
            src_ref=prod.at[s, c], dst_ref=xr.at[slot], send_sem=xs_.at[s], recv_sem=xr_.at[slot],
            device_id=device((x + dx) % 4, yh, c, z, yl), device_id_type=MESH,
        )

    def x_arrive(slot):
        pltpu.make_async_remote_copy(
            src_ref=xr.at[slot], dst_ref=xr.at[slot], send_sem=xs_.at[0], recv_sem=xr_.at[slot],
            device_id=sibling, device_id_type=MESH,
        ).wait_recv()

    y_copy = pltpu.make_async_remote_copy(
        src_ref=ys, dst_ref=yr, send_sem=ysem.at[0], recv_sem=ysem.at[1],
        device_id=device(x, 1 - yh, c, z, yl), device_id_type=MESH,
    )

    group1 = [
        ((x + dx) % 4, (c + dc) % 2, (dx * 2 + dc)) for dx in range(4) for dc in range(2) if dx or dc
    ]
    y = yh * 2 + yl
    group2 = [
        ((y + dy) % 4, (z + dz) % 4, (dy * 4 + dz)) for dy in range(4) for dz in range(4) if dy or dz
    ]

    def one_copy(px, pc, slot):
        return pltpu.make_async_remote_copy(
            src_ref=one.at[0], dst_ref=one.at[slot], send_sem=s1.at[slot], recv_sem=r1.at[slot],
            device_id=device(px, yh, pc, z, yl), device_id_type=MESH,
        )

    def two_copy(py, pz, slot):
        return pltpu.make_async_remote_copy(
            src_ref=two.at[0], dst_ref=two.at[slot], send_sem=s2.at[slot], recv_sem=r2.at[slot],
            device_id=device(x, py // 2, c, pz, py % 2), device_id_type=MESH,
        )

    for s in range(PARTS):
        for h in range(2):
            own_copy(s, h).start()
        if s == 0:
            ctx_copy.start()
    for s in range(PARTS):
        for h in range(2):
            w_copy(s, h).start()
    first_copy.start()
    second_copy.start()

    barrier = pltpu.get_barrier_semaphore()
    for px, pc, _ in group1:
        pl.semaphore_signal(barrier, inc=1, device_id=device(px, yh, pc, z, yl), device_id_type=MESH)
    for py, pz, _ in group2:
        pl.semaphore_signal(barrier, inc=1, device_id=device(x, py // 2, c, pz, py % 2), device_id_type=MESH)
    pl.semaphore_wait(barrier, len(group1) + len(group2))

    stage_a(0)
    ctx_copy.wait()
    for k in range(cx.shape[0] // 128):
        cxt[:, k * 128 : (k + 1) * 128] = cx[k * 128 : (k + 1) * 128, :].T

    def product(s, lo, hi):
        for start in range(lo, hi, 256):
            width = min(256, hi - start)
            value = jnp.dot(cxt[...], gath[s, :, start : start + width], preferred_element_type=F32)
            value = (value * multiplier).astype(BF16)
            for k in range(0, width, 128):
                column = start + k
                prod[s, column // half, :, column % half : column % half + 128] = value[:, k : k + 128]

    def context_part(s, final):
        if not final:
            for h in range(2):
                w_copy(s, h).wait()

        @pl.loop(0, acc.shape[1] // 256)
        def _(n):
            cols = pl.ds(pl.multiple_of(n * 256, 256), 256)
            value = jnp.dot(gath[s], wv[s, :, cols], preferred_element_type=F32)
            if final:
                cg[:, cols] = ((acc[:, cols] + value) * multiplier).astype(BF16)
            else:
                acc[:, cols] += value

    def whole(s):
        arrive(s, 5, 7, 8)
        by_parity(s, lambda k: arrive(s, k))
        arrive(s, 11)
        product(s, 0, 2 * half)
        core_copy(s).start()

    def cores_sum(s):
        core_copy(s).wait_recv()

        @pl.when(s % 4 != 3)
        def _():
            prod[s, c] = (prod[s, c].astype(F32) + cr[s].astype(F32)).astype(BF16)
            x_copy(s).start()

    acc[...] = jnp.zeros_like(acc)

    @pl.loop(0, last)
    def _(i):
        stage_a(i + 1)
        stage_b(i)

        @pl.when(i > 0)
        def _():
            stage_c(i - 1)

        @pl.when(i > 1)
        def _():
            s = i - 2
            whole(s)
            context_part(s, False)
            cores_sum(s)

            @pl.when(s == 4)
            def _():
                total = prod[3, c].astype(F32) + cr[3].astype(F32)
                for slot in range(3, 6):
                    x_arrive(slot)
                    total += xr[slot].astype(F32)
                ys[...] = total.astype(BF16)
                y_copy.start()

    arrive(last, 2, 0, 1)
    send(last, 3, 4, 5, 7, 6, 8, part=0)
    send(last, 3, 4, 5, 7, 6, 8, part=1)
    stage_c(last - 1)
    whole(last - 2)
    context_part(last - 2, False)
    cores_sum(last - 2)
    arrive(last, 3, 4, part=0)
    send(last, 12, 13, part=0)
    arrive(last, 6, part=0)
    send(last, 11, part=0)
    whole(last - 1)
    arrive(last, 3, 4, part=1)
    send(last, 12, 13, part=1)
    arrive(last, 6, part=1)
    send(last, 11, part=1)
    cores_sum(last - 1)
    arrive(last, 5, 7, 8, 12, 13, 11, part=0)
    product(last, 0, half)
    core_copy(last, 0).start()
    y_copy.wait_recv()
    for slot in range(3):
        x_arrive(slot)
    core_copy(last, 0).wait_recv()
    for k in range(half // 128):
        cols = slice(k * 128, (k + 1) * 128)
        total = yr[:, cols].astype(F32) + cr[last, :, cols].astype(F32)
        for slot in range(3):
            total += xr[slot, :, cols].astype(F32)
        base[cols, :] = total.T
    first_copy.wait()
    second_copy.wait()
    for h in range(2):
        w_copy(last, h).wait()
    arrive(last, 5, 7, 8, 12, 13, 11, part=1)

    def fold(value):
        total = value[0:8, 0:128]
        for r in range(value.shape[0] // 8):
            for k in range(value.shape[1] // 128):
                if r or k:
                    total += value[r * 8 : (r + 1) * 8, k * 128 : (k + 1) * 128]
        return total[0:4] + total[4:8]

    u_sum, w_sum = jnp.zeros((4, 128), F32), jnp.zeros((4, 128), F32)
    for k in range(half // 128):
        cols = slice(k * 128, (k + 1) * 128)
        at = slice(half + k * 128, half + (k + 1) * 128)
        mine = jnp.dot(cxt[...], gath[last, :, at], preferred_element_type=F32) * multiplier
        g = base[cols, :] + mine.T
        w = wv[last, at, :].astype(F32)
        m = 0.9 * mo[cols, :] + 0.1 * g
        v = 0.95 * va[cols, :] + 0.05 * g * g
        u = m / (jnp.sqrt(v) + 1e-06) + 0.1 * w
        mo[cols, :] = m
        va[cols, :] = v
        up[cols, :] = u
        u_sum += fold(u * u)
        w_sum += fold(w * w)
    one[0, 0:4] = u_sum
    one[0, 4:8] = w_sum
    for px, pc, slot in group1:
        one_copy(px, pc, slot).start()
    context_part(last - 1, False)
    for px, pc, slot in group1:
        one_copy(px, pc, slot).wait_recv()
    total = one[0]
    for _, _, slot in group1:
        total += one[slot]
    two[0] = total
    for py, pz, slot in group2:
        two_copy(py, pz, slot).start()
    context_part(last, True)

    @pl.loop(0, PARTS)
    def _(s):
        for k in range(3):
            message(s, k, False).wait_send()

        @pl.when(s < last)
        def _():
            for k in (3, 4, 5, 6, 7, 8, 11):
                message(s, k, False).wait_send()
            by_parity(s, lambda k: message(s, k, False).wait_send())
            core_copy(s).wait_send()

        @pl.when(s % 4 != 3)
        def _():
            x_copy(s).wait_send()

    for part in range(2):
        for k in (3, 4, 5, 6, 7, 8, 11, 12, 13):
            message(last, k, False, part).wait_send()
    core_copy(last, 0).wait_send()
    y_copy.wait_send()
    for px, pc, slot in group1:
        one_copy(px, pc, slot).wait_send()
    for py, pz, slot in group2:
        two_copy(py, pz, slot).wait_recv()
    total = two[0]
    for _, _, slot in group2:
        total += two[slot]
    sums[...] = total
    for py, pz, slot in group2:
        two_copy(py, pz, slot).wait_send()


def finish(cg, mo, va, up, sums, cg_out, mo_out, va_out, la_out, la, sem):
    copies = [
        pltpu.make_async_copy(src, dst, sem.at[k])
        for k, (src, dst) in enumerate(((cg, cg_out), (mo, mo_out), (va, va_out)))
    ]
    for copy in copies:
        copy.start()
    u_total = jnp.sum(sums[0:4, :], keepdims=True)
    w_total = jnp.sum(sums[4:8, :], keepdims=True)
    la[...] = up[...] * (jnp.sqrt(w_total) / jnp.sqrt(u_total + 1e-06))
    copies.append(pltpu.make_async_copy(la, la_out, sem.at[3]))
    copies[-1].start()
    for copy in copies:
        copy.wait()


def shards(context, cotangent, weight, first_moment, second_moment):
    multiplier = 1.0 / math.sqrt(HEADS * HD)
    tokens, inner = context.shape
    rows, model = cotangent.shape
    part = model // PARTS
    half = part // 2
    sem = pltpu.SemaphoreType.DMA
    n = SLOTS
    scratch = [
        pltpu.VMEM((PARTS, tokens, part), BF16),
        pltpu.VMEM((PARTS, part, inner), BF16),
        pltpu.VMEM((tokens, inner), BF16),
        pltpu.VMEM((inner, tokens), BF16),
        pltpu.VMEM((PARTS, 2, inner, half), BF16),
        pltpu.VMEM((PARTS, inner, half), BF16),
        pltpu.VMEM((6, inner, half), BF16),
        pltpu.VMEM((inner, half), BF16),
        pltpu.VMEM((inner, half), BF16),
        pltpu.VMEM((tokens, inner), F32),
        pltpu.VMEM((half, inner), F32),
        pltpu.VMEM((8, 8, 128), F32),
        pltpu.VMEM((16, 8, 128), F32),
        sem((PARTS, 2)),
        sem((PARTS, 2)),
        sem((3,)),
        sem((PARTS, n)),
        sem((PARTS, n)),
        sem((2, n)),
        sem((2, n)),
        sem((PARTS,)),
        sem((PARTS,)),
        sem((PARTS,)),
        sem((6,)),
        sem((2,)),
        sem((8,)),
        sem((8,)),
        sem((16,)),
        sem((16,)),
    ]
    vmem = pl.BlockSpec(memory_space=pltpu.VMEM)
    anywhere = pl.BlockSpec(memory_space=pl.ANY)
    state = pltpu.VMEM(first_moment.shape, F32)
    results = pl.pallas_call(
        functools.partial(kernel, multiplier),
        out_shape=(pltpu.VMEM(context.shape, BF16), state, state, state, pltpu.VMEM((8, 128), F32)),
        in_specs=[anywhere] * 5,
        out_specs=[vmem] * 5,
        scratch_shapes=scratch,
        compiler_params=pltpu.CompilerParams(
            collective_id=0, has_side_effects=True, vmem_limit_bytes=56 * 2**20
        ),
        cost_estimate=pl.CostEstimate(
            flops=4 * tokens * inner * model, bytes_accessed=40 * 2**20, transcendentals=0
        ),
        name="step",
    )(cotangent, context, weight, first_moment, second_moment)
    results = [pltpu.with_memory_space_constraint(r, pltpu.VMEM) for r in results]
    state = jax.ShapeDtypeStruct(first_moment.shape, F32)
    return pl.pallas_call(
        finish,
        out_shape=(jax.ShapeDtypeStruct(context.shape, BF16), state, state, state),
        in_specs=[vmem] * 5,
        out_specs=[anywhere] * 4,
        scratch_shapes=[pltpu.VMEM(first_moment.shape, F32), sem((4,))],
        compiler_params=pltpu.CompilerParams(vmem_limit_bytes=4 * 2**20),
        name="finish",
    )(*results)


def solution(mesh):
    in_specs = (
        P("dp", "tensor"),
        P(("dp", "tensor"), None),
        P(None, "tensor"),
        P("dp", "tensor"),
        P("dp", "tensor"),
    )
    out_specs = (P("dp", "tensor"), P("dp", "tensor"), P("dp", "tensor"), P("dp", "tensor"))
    return jax.shard_map(shards, mesh=mesh, in_specs=in_specs, out_specs=out_specs, check_vma=False)
```

```python
import functools
import math

import jax
import jax.numpy as jnp
from jax import lax
from jax.experimental import pallas as pl
from jax.experimental.pallas import tpu as pltpu
from jax.sharding import PartitionSpec as P

HEADS = 48
HD = 128
MESH = pl.DeviceIdType.MESH
PARTS = 8
F32 = jnp.float32
BF16 = jnp.bfloat16

MESSAGES = (
    ("z+", 0, 0),
    ("z-", 0, 0),
    ("y", 0, 0),
    ("z+", 0, 1),
    ("z-", 0, 1),
    ("z+", 3, 0),
    ("z-", 1, 0),
    ("y", 3, 0),
    ("y", 1, 0),
    ("z+", 3, 1),
    ("z-", 1, 1),
    ("y", 2, 0),
)
PLAN = ((64, 32), (64, 32), (64, 32), (64, 32), (96, 48), (112, 64), (112, 48), (80, 32))


def span(k, plan):
    first, plus = plan
    return ((0, 128), (0, first), (0, 64), (64, 128), (first, 128), (0, plus), (plus, first))[
        (0, 0, 0, 1, 1, 2, 3, 4, 4, 5, 6, 4)[k]
    ]


def kernel(
    multiplier,
    cot, ctx, weight, first, second,
    cg, mo, va, up, sums,
    gath, wv, cx, cxt, prod, cr, xr, ys, yr, acc, base, one, two,
    own_sem, w_sem, in_sem, gs, gr, gs7, gr7, ds_, dr, xs_, xr_, ysem, s1, r1, s2, r2,
):
    d, t = lax.axis_index("dp"), lax.axis_index("tensor")
    x, yh, c = d // 4, (d // 2) % 2, d % 2
    z, yl = t // 2, t % 2
    half = gath.shape[2] // 2
    rows = cot.shape[0]
    last = PARTS - 1

    def device(x, yh, c, z, yl):
        return ((x * 2 + yh) * 2 + c, z * 2 + yl)

    links = {
        "z+": device(x, yh, c, (z + 1) % 4, yl),
        "z-": device(x, yh, c, (z + 3) % 4, yl),
        "y": device(x, yh, c, z, 1 - yl),
    }
    sibling = device(x, yh, 1 - c, z, yl)

    def offset(s, h):
        r = s % 4
        return ((2 + 3 * r + 3 * (r * (r - 1) // 2)) * (1 + 2 * h)) % 4

    def owner(s, h):
        oy = (yh + 1 - s // 4) % 2
        h = (h + (1 - c) * (s // last)) % 2
        return (((x + offset(s, h)) % 4) * 2 + oy) * 2 + h

    def own_copy(s, h):
        at = pl.multiple_of(owner(s, h) * half, 128)
        return pltpu.make_async_copy(
            cot.at[:, pl.ds(at, half)],
            gath.at[s, pl.ds(pl.multiple_of(t * rows, rows), rows), pl.ds(h * half, half)],
            own_sem.at[s, h],
        )

    def w_copy(s, h):
        at = pl.multiple_of(owner(s, h) * half, 128)
        return pltpu.make_async_copy(
            weight.at[pl.ds(at, half)], wv.at[s, pl.ds(h * half, half)], w_sem.at[s, h]
        )

    ctx_copy = pltpu.make_async_copy(ctx, cx, in_sem.at[0])
    first_copy = pltpu.make_async_copy(first, mo, in_sem.at[1])
    second_copy = pltpu.make_async_copy(second, va, in_sem.at[2])

    def message(s, k, received, plan, part=None):
        link, dz, yb = MESSAGES[k]
        lo, hi = span(k, plan)
        if received:
            dz = (dz + {"z+": 3, "z-": 1, "y": 0}[link]) % 4
            yb = 1 - yb if link == "y" else yb
        block = ((z + dz) % 4) * 2 + (1 - yl if yb else yl)
        at = pl.ds(pl.multiple_of(block * rows + lo, 16), hi - lo)
        if part is None:
            ref, sent, got = gath.at[s, at], gs.at[s, k], gr.at[s, k]
        else:
            ref = gath.at[s, at, pl.ds(part * half, half)]
            sent, got = gs7.at[part, k], gr7.at[part, k]
        return pltpu.make_async_remote_copy(
            src_ref=ref, dst_ref=ref, send_sem=sent, recv_sem=got,
            device_id=links[link], device_id_type=MESH,
        )

    def by_plan(s, action):
        if isinstance(s, int):
            action(PLAN[s])
            return
        lo = 0
        for hi in range(1, last + 1):
            if hi == last or PLAN[hi] != PLAN[lo]:

                @pl.when((s >= lo) & (s < hi))
                def _(plan=PLAN[lo]):
                    action(plan)

                lo = hi

    def send(s, plan, *ks, part=None):
        for k in ks:
            message(s, k, False, plan, part).start()

    def arrive(s, plan, *ks, part=None):
        for k in ks:
            message(s, k, True, plan, part).wait_recv()

    def stage_a(s):
        for h in range(2):
            own_copy(s, h).wait()
        send(s, PLAN[0], 0, 1, 2)

    def stage_b(s, part=None, first=True):
        def steps(plan):
            if first:
                arrive(s, plan, 2)
            send(s, plan, 3, 4, part=part)
            if first:
                arrive(s, plan, 0)
            send(s, plan, 5, 7, part=part)
            if first:
                arrive(s, plan, 1)
            send(s, plan, 6, 8, part=part)

        by_plan(s, steps)

    def stage_c(s, part=None):
        def steps(plan):
            arrive(s, plan, 3, part=part)
            send(s, plan, 9, part=part)
            arrive(s, plan, 4, part=part)
            send(s, plan, 10, part=part)
            arrive(s, plan, 6, part=part)
            send(s, plan, 11, part=part)

        by_plan(s, steps)

    def gathered(s, part=None):
        by_plan(s, lambda plan: arrive(s, plan, 5, 7, 8, 9, 10, 11, part=part))

    def core_copy(s, part=None):
        src = prod.at[s, 1 - c] if part is None else prod.at[s, part]
        return pltpu.make_async_remote_copy(
            src_ref=src, dst_ref=cr.at[s], send_sem=ds_.at[s], recv_sem=dr.at[s],
            device_id=sibling, device_id_type=MESH,
        )

    def x_copy(s):
        dx = offset(s, c)
        slot = (1 - s // 4) * 3 + (dx + 3) % 4
        return pltpu.make_async_remote_copy(
            src_ref=prod.at[s, c], dst_ref=xr.at[slot], send_sem=xs_.at[s], recv_sem=xr_.at[slot],
            device_id=device((x + dx) % 4, yh, c, z, yl), device_id_type=MESH,
        )

    def x_arrive(slot):
        pltpu.make_async_remote_copy(
            src_ref=xr.at[slot], dst_ref=xr.at[slot], send_sem=xs_.at[0], recv_sem=xr_.at[slot],
            device_id=sibling, device_id_type=MESH,
        ).wait_recv()

    y_copy = pltpu.make_async_remote_copy(
        src_ref=ys, dst_ref=yr, send_sem=ysem.at[0], recv_sem=ysem.at[1],
        device_id=device(x, 1 - yh, c, z, yl), device_id_type=MESH,
    )

    group1 = [
        ((x + dx) % 4, (c + dc) % 2, (dx * 2 + dc)) for dx in range(4) for dc in range(2) if dx or dc
    ]
    y = yh * 2 + yl
    group2 = [
        ((y + dy) % 4, (z + dz) % 4, (dy * 4 + dz)) for dy in range(4) for dz in range(4) if dy or dz
    ]

    def one_copy(px, pc, slot):
        return pltpu.make_async_remote_copy(
            src_ref=one.at[0], dst_ref=one.at[slot], send_sem=s1.at[slot], recv_sem=r1.at[slot],
            device_id=device(px, yh, pc, z, yl), device_id_type=MESH,
        )

    def two_copy(py, pz, slot):
        return pltpu.make_async_remote_copy(
            src_ref=two.at[0], dst_ref=two.at[slot], send_sem=s2.at[slot], recv_sem=r2.at[slot],
            device_id=device(x, py // 2, c, pz, py % 2), device_id_type=MESH,
        )

    for s in range(PARTS):
        for h in range(2):
            own_copy(s, h).start()
        if s == 0:
            ctx_copy.start()
    for s in range(PARTS):
        for h in range(2):
            w_copy(s, h).start()
    first_copy.start()
    second_copy.start()

    barrier = pltpu.get_barrier_semaphore()
    for px, pc, _ in group1:
        pl.semaphore_signal(barrier, inc=1, device_id=device(px, yh, pc, z, yl), device_id_type=MESH)
    for py, pz, _ in group2:
        pl.semaphore_signal(barrier, inc=1, device_id=device(x, py // 2, c, pz, py % 2), device_id_type=MESH)
    pl.semaphore_wait(barrier, len(group1) + len(group2))

    stage_a(0)
    ctx_copy.wait()
    for k in range(cx.shape[0] // 128):
        cxt[:, k * 128 : (k + 1) * 128] = cx[k * 128 : (k + 1) * 128, :].T

    def product(s, lo, hi):
        for start in range(lo, hi, 256):
            width = min(256, hi - start)
            value = jnp.dot(cxt[...], gath[s, :, start : start + width], preferred_element_type=F32)
            value = (value * multiplier).astype(BF16)
            for k in range(0, width, 128):
                column = start + k
                prod[s, column // half, :, column % half : column % half + 128] = value[:, k : k + 128]

    def context_part(s, final):
        if not final:
            for h in range(2):
                w_copy(s, h).wait()

        @pl.loop(0, acc.shape[1] // 256)
        def _(n):
            cols = pl.ds(pl.multiple_of(n * 256, 256), 256)
            value = jnp.dot(gath[s], wv[s, :, cols], preferred_element_type=F32)
            if final:
                cg[:, cols] = ((acc[:, cols] + value) * multiplier).astype(BF16)
            else:
                acc[:, cols] += value

    def whole(s):
        gathered(s)
        product(s, 0, 2 * half)
        core_copy(s).start()

    def cores_sum(s):
        core_copy(s).wait_recv()

        @pl.when(s % 4 != 3)
        def _():
            prod[s, c] = (prod[s, c].astype(F32) + cr[s].astype(F32)).astype(BF16)
            x_copy(s).start()

    acc[...] = jnp.zeros_like(acc)

    @pl.loop(0, last)
    def _(i):
        @pl.when(i < last - 1)
        def _():
            stage_a(i + 1)

        stage_b(i)

        @pl.when(i > 0)
        def _():
            stage_c(i - 1)

        @pl.when(i == last - 1)
        def _():
            stage_a(last)

        @pl.when(i > 1)
        def _():
            s = i - 2
            whole(s)
            context_part(s, False)
            cores_sum(s)

            @pl.when(s == 3)
            def _():
                total = prod[3, c].astype(F32) + cr[3].astype(F32)
                for slot in range(3, 6):
                    x_arrive(slot)
                    total += xr[slot].astype(F32)
                ys[...] = total.astype(BF16)
                y_copy.start()

    stage_c(last - 1)
    stage_b(last, part=0)
    stage_b(last, part=1, first=False)
    whole(last - 2)
    cores_sum(last - 2)
    whole(last - 1)
    cores_sum(last - 1)
    stage_c(last, part=0)
    stage_c(last, part=1)
    context_part(last - 2, False)
    gathered(last, part=0)
    product(last, 0, half)
    core_copy(last, 0).start()
    y_copy.wait_recv()
    for slot in range(3):
        x_arrive(slot)
    core_copy(last, 0).wait_recv()
    for k in range(half // 128):
        cols = slice(k * 128, (k + 1) * 128)
        total = yr[:, cols].astype(F32) + cr[last, :, cols].astype(F32)
        for slot in range(3):
            total += xr[slot, :, cols].astype(F32)
        base[cols, :] = total.T
    first_copy.wait()
    second_copy.wait()
    for h in range(2):
        w_copy(last, h).wait()
    gathered(last, part=1)

    def fold(value):
        total = value[0:8, 0:128]
        for r in range(value.shape[0] // 8):
            for k in range(value.shape[1] // 128):
                if r or k:
                    total += value[r * 8 : (r + 1) * 8, k * 128 : (k + 1) * 128]
        return total[0:4] + total[4:8]

    u_sum, w_sum = jnp.zeros((4, 128), F32), jnp.zeros((4, 128), F32)
    for k in range(half // 128):
        cols = slice(k * 128, (k + 1) * 128)
        at = slice(half + k * 128, half + (k + 1) * 128)
        mine = jnp.dot(cxt[...], gath[last, :, at], preferred_element_type=F32) * multiplier
        g = base[cols, :] + mine.T
        w = wv[last, at, :].astype(F32)
        m = 0.9 * mo[cols, :] + 0.1 * g
        v = 0.95 * va[cols, :] + 0.05 * g * g
        u = m / (jnp.sqrt(v) + 1e-06) + 0.1 * w
        mo[cols, :] = m
        va[cols, :] = v
        up[cols, :] = u
        u_sum += fold(u * u)
        w_sum += fold(w * w)
    one[0, 0:4] = u_sum
    one[0, 4:8] = w_sum
    for px, pc, slot in group1:
        one_copy(px, pc, slot).start()
    context_part(last - 1, False)
    for px, pc, slot in group1:
        one_copy(px, pc, slot).wait_recv()
    total = one[0]
    for _, _, slot in group1:
        total += one[slot]
    two[0] = total
    for py, pz, slot in group2:
        two_copy(py, pz, slot).start()
    context_part(last, True)

    @pl.loop(0, PARTS)
    def _(s):
        for k in range(3):
            message(s, k, False, PLAN[0]).wait_send()

        @pl.when(s < last)
        def _():
            def steps(plan):
                for k in range(3, len(MESSAGES)):
                    message(s, k, False, plan).wait_send()

            by_plan(s, steps)
            core_copy(s).wait_send()

        @pl.when(s % 4 != 3)
        def _():
            x_copy(s).wait_send()

    for part in range(2):
        for k in range(3, len(MESSAGES)):
            message(last, k, False, PLAN[last], part).wait_send()
    core_copy(last, 0).wait_send()
    y_copy.wait_send()
    for px, pc, slot in group1:
        one_copy(px, pc, slot).wait_send()
    for py, pz, slot in group2:
        two_copy(py, pz, slot).wait_recv()
    total = two[0]
    for _, _, slot in group2:
        total += two[slot]
    sums[...] = total
    for py, pz, slot in group2:
        two_copy(py, pz, slot).wait_send()


def finish(cg, mo, va, up, sums, cg_out, mo_out, va_out, la_out, la, sem):
    copies = [
        pltpu.make_async_copy(src, dst, sem.at[k])
        for k, (src, dst) in enumerate(((cg, cg_out), (mo, mo_out), (va, va_out)))
    ]
    for copy in copies:
        copy.start()
    u_total = jnp.sum(sums[0:4, :], keepdims=True)
    w_total = jnp.sum(sums[4:8, :], keepdims=True)
    la[...] = up[...] * (jnp.sqrt(w_total) / jnp.sqrt(u_total + 1e-06))
    copies.append(pltpu.make_async_copy(la, la_out, sem.at[3]))
    copies[-1].start()
    for copy in copies:
        copy.wait()


def shards(context, cotangent, weight, first_moment, second_moment):
    multiplier = 1.0 / math.sqrt(HEADS * HD)
    tokens, inner = context.shape
    rows, model = cotangent.shape
    part = model // PARTS
    half = part // 2
    sem = pltpu.SemaphoreType.DMA
    n = len(MESSAGES)
    scratch = [
        pltpu.VMEM((PARTS, tokens, part), BF16),
        pltpu.VMEM((PARTS, part, inner), BF16),
        pltpu.VMEM((tokens, inner), BF16),
        pltpu.VMEM((inner, tokens), BF16),
        pltpu.VMEM((PARTS, 2, inner, half), BF16),
        pltpu.VMEM((PARTS, inner, half), BF16),
        pltpu.VMEM((6, inner, half), BF16),
        pltpu.VMEM((inner, half), BF16),
        pltpu.VMEM((inner, half), BF16),
        pltpu.VMEM((tokens, inner), F32),
        pltpu.VMEM((half, inner), F32),
        pltpu.VMEM((8, 8, 128), F32),
        pltpu.VMEM((16, 8, 128), F32),
        sem((PARTS, 2)),
        sem((PARTS, 2)),
        sem((3,)),
        sem((PARTS, n)),
        sem((PARTS, n)),
        sem((2, n)),
        sem((2, n)),
        sem((PARTS,)),
        sem((PARTS,)),
        sem((PARTS,)),
        sem((6,)),
        sem((2,)),
        sem((8,)),
        sem((8,)),
        sem((16,)),
        sem((16,)),
    ]
    vmem = pl.BlockSpec(memory_space=pltpu.VMEM)
    anywhere = pl.BlockSpec(memory_space=pl.ANY)
    state = pltpu.VMEM(first_moment.shape, F32)
    results = pl.pallas_call(
        functools.partial(kernel, multiplier),
        out_shape=(pltpu.VMEM(context.shape, BF16), state, state, state, pltpu.VMEM((8, 128), F32)),
        in_specs=[anywhere] * 5,
        out_specs=[vmem] * 5,
        scratch_shapes=scratch,
        compiler_params=pltpu.CompilerParams(
            collective_id=0, has_side_effects=True, vmem_limit_bytes=56 * 2**20
        ),
        cost_estimate=pl.CostEstimate(
            flops=4 * tokens * inner * model, bytes_accessed=40 * 2**20, transcendentals=0
        ),
        name="step",
    )(cotangent, context, weight, first_moment, second_moment)
    results = [pltpu.with_memory_space_constraint(r, pltpu.VMEM) for r in results]
    state = jax.ShapeDtypeStruct(first_moment.shape, F32)
    return pl.pallas_call(
        finish,
        out_shape=(jax.ShapeDtypeStruct(context.shape, BF16), state, state, state),
        in_specs=[vmem] * 5,
        out_specs=[anywhere] * 4,
        scratch_shapes=[pltpu.VMEM(first_moment.shape, F32), sem((4,))],
        compiler_params=pltpu.CompilerParams(vmem_limit_bytes=4 * 2**20),
        name="finish",
    )(*results)


def solution(mesh):
    in_specs = (
        P("dp", "tensor"),
        P(("dp", "tensor"), None),
        P(None, "tensor"),
        P("dp", "tensor"),
        P("dp", "tensor"),
    )
    out_specs = (P("dp", "tensor"), P("dp", "tensor"), P("dp", "tensor"), P("dp", "tensor"))
    return jax.shard_map(shards, mesh=mesh, in_specs=in_specs, out_specs=out_specs, check_vma=False)
```

```python
import functools
import math

import jax
import jax.numpy as jnp
from jax import lax
from jax.experimental import pallas as pl
from jax.experimental.pallas import tpu as pltpu
from jax.sharding import PartitionSpec as P

HEADS = 48
HD = 128
MESH = pl.DeviceIdType.MESH
PARTS = 8
F32 = jnp.float32
BF16 = jnp.bfloat16

MESSAGES = (
    ("z+", 0, 0),
    ("z-", 0, 0),
    ("y", 0, 0),
    ("z+", 0, 1),
    ("z-", 0, 1),
    ("z+", 3, 0),
    ("z-", 1, 0),
    ("y", 3, 0),
    ("y", 1, 0),
    ("z+", 3, 1),
    ("z-", 1, 1),
    ("y", 2, 0),
)
PLAN = ((64, 32), (64, 32), (64, 32), (64, 32), (96, 48), (112, 64), (112, 48), (80, 32))


def span(k, plan):
    first, plus = plan
    return ((0, 128), (0, first), (0, 64), (64, 128), (first, 128), (0, plus), (plus, first))[
        (0, 0, 0, 1, 1, 2, 3, 4, 4, 5, 6, 4)[k]
    ]


def kernel(
    multiplier,
    cot, ctx, weight, first, second,
    cg, mo, va, up, sums,
    gath, wv, cx, cxt, prod, cr, xr, ys, yr, acc, mine, one, two,
    own_sem, w_sem, in_sem, gs, gr, gs7, gr7, ds_, dr, xs_, xr_, ysem, s1, r1, s2, r2,
):
    d, t = lax.axis_index("dp"), lax.axis_index("tensor")
    x, yh, c = d // 4, (d // 2) % 2, d % 2
    z, yl = t // 2, t % 2
    half = gath.shape[2] // 2
    rows = cot.shape[0]
    last = PARTS - 1

    def device(x, yh, c, z, yl):
        return ((x * 2 + yh) * 2 + c, z * 2 + yl)

    links = {
        "z+": device(x, yh, c, (z + 1) % 4, yl),
        "z-": device(x, yh, c, (z + 3) % 4, yl),
        "y": device(x, yh, c, z, 1 - yl),
    }
    sibling = device(x, yh, 1 - c, z, yl)

    def offset(s, h):
        r = s % 4
        return ((2 + 3 * r + 3 * (r * (r - 1) // 2)) * (1 + 2 * h)) % 4

    def owner(s, h):
        oy = (yh + 1 - s // 4) % 2
        h = (h + (1 - c) * (s // last)) % 2
        return (((x + offset(s, h)) % 4) * 2 + oy) * 2 + h

    def own_copy(s, h):
        at = pl.multiple_of(owner(s, h) * half, 128)
        return pltpu.make_async_copy(
            cot.at[:, pl.ds(at, half)],
            gath.at[s, pl.ds(pl.multiple_of(t * rows, rows), rows), pl.ds(h * half, half)],
            own_sem.at[s, h],
        )

    def w_copy(s, h):
        at = pl.multiple_of(owner(s, h) * half, 128)
        return pltpu.make_async_copy(
            weight.at[pl.ds(at, half)], wv.at[s, pl.ds(h * half, half)], w_sem.at[s, h]
        )

    ctx_copy = pltpu.make_async_copy(ctx, cx, in_sem.at[0])
    first_copy = pltpu.make_async_copy(first, mo, in_sem.at[1])
    second_copy = pltpu.make_async_copy(second, va, in_sem.at[2])

    def message(s, k, received, plan, part=None):
        link, dz, yb = MESSAGES[k]
        lo, hi = span(k, plan)
        if received:
            dz = (dz + {"z+": 3, "z-": 1, "y": 0}[link]) % 4
            yb = 1 - yb if link == "y" else yb
        block = ((z + dz) % 4) * 2 + (1 - yl if yb else yl)
        at = pl.ds(pl.multiple_of(block * rows + lo, 16), hi - lo)
        if part is None:
            ref, sent, got = gath.at[s, at], gs.at[s, k], gr.at[s, k]
        else:
            ref = gath.at[s, at, pl.ds(part * half, half)]
            sent, got = gs7.at[part, k], gr7.at[part, k]
        return pltpu.make_async_remote_copy(
            src_ref=ref, dst_ref=ref, send_sem=sent, recv_sem=got,
            device_id=links[link], device_id_type=MESH,
        )

    def by_plan(s, action):
        if isinstance(s, int):
            action(PLAN[s])
            return
        lo = 0
        for hi in range(1, last + 1):
            if hi == last or PLAN[hi] != PLAN[lo]:

                @pl.when((s >= lo) & (s < hi))
                def _(plan=PLAN[lo]):
                    action(plan)

                lo = hi

    def send(s, plan, *ks, part=None):
        for k in ks:
            message(s, k, False, plan, part).start()

    def arrive(s, plan, *ks, part=None):
        for k in ks:
            message(s, k, True, plan, part).wait_recv()

    def stage_a(s):
        for h in range(2):
            own_copy(s, h).wait()
        send(s, PLAN[0], 0, 1, 2)

    def stage_b(s, part=None, first=True):
        def steps(plan):
            if first:
                arrive(s, plan, 2)
            send(s, plan, 3, 4, part=part)
            if first:
                arrive(s, plan, 0)
            send(s, plan, 5, 7, part=part)
            if first:
                arrive(s, plan, 1)
            send(s, plan, 6, 8, part=part)

        by_plan(s, steps)

    def stage_c(s, part=None):
        def steps(plan):
            arrive(s, plan, 3, part=part)
            send(s, plan, 9, part=part)
            arrive(s, plan, 4, part=part)
            send(s, plan, 10, part=part)
            arrive(s, plan, 6, part=part)
            send(s, plan, 11, part=part)

        by_plan(s, steps)

    def gathered(s, part=None):
        by_plan(s, lambda plan: arrive(s, plan, 5, 7, 8, 9, 10, 11, part=part))

    def core_copy(s, part=None):
        src = prod.at[s, 1 - c] if part is None else prod.at[s, part]
        return pltpu.make_async_remote_copy(
            src_ref=src, dst_ref=cr.at[s], send_sem=ds_.at[s], recv_sem=dr.at[s],
            device_id=sibling, device_id_type=MESH,
        )

    def x_copy(s):
        dx = offset(s, c)
        slot = (1 - s // 4) * 3 + (dx + 3) % 4
        return pltpu.make_async_remote_copy(
            src_ref=prod.at[s, c], dst_ref=xr.at[slot], send_sem=xs_.at[s], recv_sem=xr_.at[slot],
            device_id=device((x + dx) % 4, yh, c, z, yl), device_id_type=MESH,
        )

    def x_arrive(slot):
        pltpu.make_async_remote_copy(
            src_ref=xr.at[slot], dst_ref=xr.at[slot], send_sem=xs_.at[0], recv_sem=xr_.at[slot],
            device_id=sibling, device_id_type=MESH,
        ).wait_recv()

    y_copy = pltpu.make_async_remote_copy(
        src_ref=ys, dst_ref=yr, send_sem=ysem.at[0], recv_sem=ysem.at[1],
        device_id=device(x, 1 - yh, c, z, yl), device_id_type=MESH,
    )

    group1 = [
        ((x + dx) % 4, (c + dc) % 2, (dx * 2 + dc)) for dx in range(4) for dc in range(2) if dx or dc
    ]
    y = yh * 2 + yl
    group2 = [
        ((y + dy) % 4, (z + dz) % 4, (dy * 4 + dz)) for dy in range(4) for dz in range(4) if dy or dz
    ]

    def one_copy(px, pc, slot):
        return pltpu.make_async_remote_copy(
            src_ref=one.at[0], dst_ref=one.at[slot], send_sem=s1.at[slot], recv_sem=r1.at[slot],
            device_id=device(px, yh, pc, z, yl), device_id_type=MESH,
        )

    def two_copy(py, pz, slot):
        return pltpu.make_async_remote_copy(
            src_ref=two.at[0], dst_ref=two.at[slot], send_sem=s2.at[slot], recv_sem=r2.at[slot],
            device_id=device(x, py // 2, c, pz, py % 2), device_id_type=MESH,
        )

    for s in range(PARTS):
        for h in range(2):
            own_copy(s, h).start()
        if s == 0:
            ctx_copy.start()
    for s in range(PARTS):
        for h in range(2):
            w_copy(s, h).start()
    first_copy.start()
    second_copy.start()

    barrier = pltpu.get_barrier_semaphore()
    for px, pc, _ in group1:
        pl.semaphore_signal(barrier, inc=1, device_id=device(px, yh, pc, z, yl), device_id_type=MESH)
    for py, pz, _ in group2:
        pl.semaphore_signal(barrier, inc=1, device_id=device(x, py // 2, c, pz, py % 2), device_id_type=MESH)
    pl.semaphore_wait(barrier, len(group1) + len(group2))

    stage_a(0)
    ctx_copy.wait()
    for k in range(cx.shape[0] // 128):
        cxt[:, k * 128 : (k + 1) * 128] = cx[k * 128 : (k + 1) * 128, :].T

    def product(s, lo, hi):
        for start in range(lo, hi, 256):
            width = min(256, hi - start)
            value = jnp.dot(cxt[...], gath[s, :, start : start + width], preferred_element_type=F32)
            value = (value * multiplier).astype(BF16)
            for k in range(0, width, 128):
                column = start + k
                prod[s, column // half, :, column % half : column % half + 128] = value[:, k : k + 128]

    def context_part(s, final):
        if not final:
            for h in range(2):
                w_copy(s, h).wait()

        @pl.loop(0, acc.shape[1] // 256)
        def _(n):
            cols = pl.ds(pl.multiple_of(n * 256, 256), 256)
            value = jnp.dot(gath[s], wv[s, :, cols], preferred_element_type=F32)
            if final:
                cg[:, cols] = ((acc[:, cols] + value) * multiplier).astype(BF16)
            else:
                acc[:, cols] += value

    def whole(s):
        gathered(s)
        product(s, 0, 2 * half)
        core_copy(s).start()

    def cores_sum(s):
        core_copy(s).wait_recv()

        @pl.when(s % 4 != 3)
        def _():
            prod[s, c] = (prod[s, c].astype(F32) + cr[s].astype(F32)).astype(BF16)
            x_copy(s).start()

    acc[...] = jnp.zeros_like(acc)

    @pl.loop(0, last)
    def _(i):
        @pl.when(i < last - 1)
        def _():
            stage_a(i + 1)

        stage_b(i)

        @pl.when(i > 0)
        def _():
            stage_c(i - 1)

        @pl.when(i == last - 1)
        def _():
            stage_a(last)

        @pl.when(i > 1)
        def _():
            s = i - 2
            whole(s)
            context_part(s, False)
            cores_sum(s)

            @pl.when(s == 3)
            def _():
                total = prod[3, c].astype(F32) + cr[3].astype(F32)
                for slot in range(3, 6):
                    x_arrive(slot)
                    total += xr[slot].astype(F32)
                ys[...] = total.astype(BF16)
                y_copy.start()

    whole(last - 2)
    stage_c(last - 1)
    cores_sum(last - 2)
    stage_b(last, part=0)
    stage_b(last, part=1, first=False)
    whole(last - 1)
    cores_sum(last - 1)
    stage_c(last, part=0)
    stage_c(last, part=1)
    gathered(last, part=0)
    product(last, 0, half)
    core_copy(last, 0).start()
    gathered(last, part=1)
    for start, width in ((0, 256), (256, 128)):
        value = jnp.dot(cxt[...], gath[last, :, half + start : half + start + width], preferred_element_type=F32)
        mine[:, start : start + width] = value * multiplier
    context_part(last - 2, False)
    y_copy.wait_recv()
    for slot in range(3):
        x_arrive(slot)
    core_copy(last, 0).wait_recv()
    for k in range(half // 128):
        cols = slice(k * 128, (k + 1) * 128)
        total = yr[:, cols].astype(F32) + cr[last, :, cols].astype(F32)
        for slot in range(3):
            total += xr[slot, :, cols].astype(F32)
        mine[:, cols] += total
    first_copy.wait()
    second_copy.wait()
    for h in range(2):
        w_copy(last, h).wait()

    def fold(value):
        total = value[0:8, 0:128]
        for r in range(value.shape[0] // 8):
            for k in range(value.shape[1] // 128):
                if r or k:
                    total += value[r * 8 : (r + 1) * 8, k * 128 : (k + 1) * 128]
        return total[0:4] + total[4:8]

    u_sum, w_sum = jnp.zeros((4, 128), F32), jnp.zeros((4, 128), F32)
    for k in range(half // 128):
        cols = slice(k * 128, (k + 1) * 128)
        at = slice(half + k * 128, half + (k + 1) * 128)
        g = mine[:, cols].T
        w = wv[last, at, :].astype(F32)
        m = 0.9 * mo[cols, :] + 0.1 * g
        v = 0.95 * va[cols, :] + 0.05 * g * g
        u = m / (jnp.sqrt(v) + 1e-06) + 0.1 * w
        mo[cols, :] = m
        va[cols, :] = v
        up[cols, :] = u
        u_sum += fold(u * u)
        w_sum += fold(w * w)
    one[0, 0:4] = u_sum
    one[0, 4:8] = w_sum
    for px, pc, slot in group1:
        one_copy(px, pc, slot).start()
    context_part(last - 1, False)
    for px, pc, slot in group1:
        one_copy(px, pc, slot).wait_recv()
    total = one[0]
    for _, _, slot in group1:
        total += one[slot]
    two[0] = total
    for py, pz, slot in group2:
        two_copy(py, pz, slot).start()
    context_part(last, True)

    @pl.loop(0, PARTS)
    def _(s):
        for k in range(3):
            message(s, k, False, PLAN[0]).wait_send()

        @pl.when(s < last)
        def _():
            def steps(plan):
                for k in range(3, len(MESSAGES)):
                    message(s, k, False, plan).wait_send()

            by_plan(s, steps)
            core_copy(s).wait_send()

        @pl.when(s % 4 != 3)
        def _():
            x_copy(s).wait_send()

    for part in range(2):
        for k in range(3, len(MESSAGES)):
            message(last, k, False, PLAN[last], part).wait_send()
    core_copy(last, 0).wait_send()
    y_copy.wait_send()
    for px, pc, slot in group1:
        one_copy(px, pc, slot).wait_send()
    for py, pz, slot in group2:
        two_copy(py, pz, slot).wait_recv()
    total = two[0]
    for _, _, slot in group2:
        total += two[slot]
    sums[...] = total
    for py, pz, slot in group2:
        two_copy(py, pz, slot).wait_send()


def finish(cg, mo, va, up, sums, cg_out, mo_out, va_out, la_out, la, sem):
    copies = [
        pltpu.make_async_copy(src, dst, sem.at[k])
        for k, (src, dst) in enumerate(((cg, cg_out), (mo, mo_out), (va, va_out)))
    ]
    for copy in copies:
        copy.start()
    u_total = jnp.sum(sums[0:4, :], keepdims=True)
    w_total = jnp.sum(sums[4:8, :], keepdims=True)
    la[...] = up[...] * (jnp.sqrt(w_total) / jnp.sqrt(u_total + 1e-06))
    copies.append(pltpu.make_async_copy(la, la_out, sem.at[3]))
    copies[-1].start()
    for copy in copies:
        copy.wait()


def shards(context, cotangent, weight, first_moment, second_moment):
    multiplier = 1.0 / math.sqrt(HEADS * HD)
    tokens, inner = context.shape
    rows, model = cotangent.shape
    part = model // PARTS
    half = part // 2
    sem = pltpu.SemaphoreType.DMA
    n = len(MESSAGES)
    scratch = [
        pltpu.VMEM((PARTS, tokens, part), BF16),
        pltpu.VMEM((PARTS, part, inner), BF16),
        pltpu.VMEM((tokens, inner), BF16),
        pltpu.VMEM((inner, tokens), BF16),
        pltpu.VMEM((PARTS, 2, inner, half), BF16),
        pltpu.VMEM((PARTS, inner, half), BF16),
        pltpu.VMEM((6, inner, half), BF16),
        pltpu.VMEM((inner, half), BF16),
        pltpu.VMEM((inner, half), BF16),
        pltpu.VMEM((tokens, inner), F32),
        pltpu.VMEM((inner, half), F32),
        pltpu.VMEM((8, 8, 128), F32),
        pltpu.VMEM((16, 8, 128), F32),
        sem((PARTS, 2)),
        sem((PARTS, 2)),
        sem((3,)),
        sem((PARTS, n)),
        sem((PARTS, n)),
        sem((2, n)),
        sem((2, n)),
        sem((PARTS,)),
        sem((PARTS,)),
        sem((PARTS,)),
        sem((6,)),
        sem((2,)),
        sem((8,)),
        sem((8,)),
        sem((16,)),
        sem((16,)),
    ]
    vmem = pl.BlockSpec(memory_space=pltpu.VMEM)
    anywhere = pl.BlockSpec(memory_space=pl.ANY)
    state = pltpu.VMEM(first_moment.shape, F32)
    results = pl.pallas_call(
        functools.partial(kernel, multiplier),
        out_shape=(pltpu.VMEM(context.shape, BF16), state, state, state, pltpu.VMEM((8, 128), F32)),
        in_specs=[anywhere] * 5,
        out_specs=[vmem] * 5,
        scratch_shapes=scratch,
        compiler_params=pltpu.CompilerParams(
            collective_id=0, has_side_effects=True, vmem_limit_bytes=56 * 2**20
        ),
        cost_estimate=pl.CostEstimate(
            flops=4 * tokens * inner * model, bytes_accessed=40 * 2**20, transcendentals=0
        ),
        name="step",
    )(cotangent, context, weight, first_moment, second_moment)
    results = [pltpu.with_memory_space_constraint(r, pltpu.VMEM) for r in results]
    state = jax.ShapeDtypeStruct(first_moment.shape, F32)
    return pl.pallas_call(
        finish,
        out_shape=(jax.ShapeDtypeStruct(context.shape, BF16), state, state, state),
        in_specs=[vmem] * 5,
        out_specs=[anywhere] * 4,
        scratch_shapes=[pltpu.VMEM(first_moment.shape, F32), sem((4,))],
        compiler_params=pltpu.CompilerParams(vmem_limit_bytes=4 * 2**20),
        name="finish",
    )(*results)


def solution(mesh):
    in_specs = (
        P("dp", "tensor"),
        P(("dp", "tensor"), None),
        P(None, "tensor"),
        P("dp", "tensor"),
        P("dp", "tensor"),
    )
    out_specs = (P("dp", "tensor"), P("dp", "tensor"), P("dp", "tensor"), P("dp", "tensor"))
    return jax.shard_map(shards, mesh=mesh, in_specs=in_specs, out_specs=out_specs, check_vma=False)
```

```python
import functools
import math

import jax
import jax.numpy as jnp
from jax import lax
from jax.experimental import pallas as pl
from jax.experimental.pallas import tpu as pltpu
from jax.sharding import PartitionSpec as P

HEADS = 48
HD = 128
MESH = pl.DeviceIdType.MESH
PARTS = 8
F32 = jnp.float32
BF16 = jnp.bfloat16

MESSAGES = (
    ("z+", 0, 0),
    ("z-", 0, 0),
    ("y", 0, 0),
    ("z+", 0, 1),
    ("z-", 0, 1),
    ("z+", 3, 0),
    ("z-", 1, 0),
    ("y", 3, 0),
    ("y", 1, 0),
    ("z+", 3, 1),
    ("z-", 1, 1),
    ("y", 2, 0),
)
PLAN = ((64, 32), (64, 32), (64, 32), (64, 32), (96, 48), (112, 64), (112, 48), (80, 32))


def span(k, plan):
    first, plus = plan
    return ((0, 128), (0, first), (0, 64), (64, 128), (first, 128), (0, plus), (plus, first))[
        (0, 0, 0, 1, 1, 2, 3, 4, 4, 5, 6, 4)[k]
    ]


def kernel(
    multiplier,
    cot, ctx, weight, first, second,
    cg, mo, va, up, sums,
    gath, wv, cx, cxt, prod, cr, xr, ys, yr, acc, mine, one, two,
    own_sem, w_sem, in_sem, gs, gr, gs7, gr7, ds_, dr, xs_, xr_, ysem, s1, r1, s2, r2,
):
    d, t = lax.axis_index("dp"), lax.axis_index("tensor")
    x, yh, c = d // 4, (d // 2) % 2, d % 2
    z, yl = t // 2, t % 2
    half = gath.shape[2] // 2
    rows = cot.shape[0]
    last = PARTS - 1

    def device(x, yh, c, z, yl):
        return ((x * 2 + yh) * 2 + c, z * 2 + yl)

    links = {
        "z+": device(x, yh, c, (z + 1) % 4, yl),
        "z-": device(x, yh, c, (z + 3) % 4, yl),
        "y": device(x, yh, c, z, 1 - yl),
    }
    sibling = device(x, yh, 1 - c, z, yl)

    def offset(s, h):
        r = s % 4
        return ((2 + 3 * r + 3 * (r * (r - 1) // 2)) * (1 + 2 * h)) % 4

    def owner(s, h):
        oy = (yh + 1 - s // 4) % 2
        h = (h + (1 - c) * (s // last)) % 2
        return (((x + offset(s, h)) % 4) * 2 + oy) * 2 + h

    def own_copy(s, h):
        at = pl.multiple_of(owner(s, h) * half, 128)
        return pltpu.make_async_copy(
            cot.at[:, pl.ds(at, half)],
            gath.at[s, pl.ds(pl.multiple_of(t * rows, rows), rows), pl.ds(h * half, half)],
            own_sem.at[s, h],
        )

    def w_copy(s, h):
        at = pl.multiple_of(owner(s, h) * half, 128)
        return pltpu.make_async_copy(
            weight.at[pl.ds(at, half)], wv.at[s, pl.ds(h * half, half)], w_sem.at[s, h]
        )

    ctx_copy = pltpu.make_async_copy(ctx, cx, in_sem.at[0])
    first_copy = pltpu.make_async_copy(first, mo, in_sem.at[1])
    second_copy = pltpu.make_async_copy(second, va, in_sem.at[2])

    def message(s, k, received, plan, part=None):
        link, dz, yb = MESSAGES[k]
        lo, hi = span(k, plan)
        if received:
            dz = (dz + {"z+": 3, "z-": 1, "y": 0}[link]) % 4
            yb = 1 - yb if link == "y" else yb
        block = ((z + dz) % 4) * 2 + (1 - yl if yb else yl)
        at = pl.ds(pl.multiple_of(block * rows + lo, 16), hi - lo)
        if part is None:
            ref, sent, got = gath.at[s, at], gs.at[s, k], gr.at[s, k]
        else:
            ref = gath.at[s, at, pl.ds(part * half, half)]
            sent, got = gs7.at[part, k], gr7.at[part, k]
        return pltpu.make_async_remote_copy(
            src_ref=ref, dst_ref=ref, send_sem=sent, recv_sem=got,
            device_id=links[link], device_id_type=MESH,
        )

    def by_plan(s, action):
        if isinstance(s, int):
            action(PLAN[s])
            return
        lo = 0
        for hi in range(1, last + 1):
            if hi == last or PLAN[hi] != PLAN[lo]:

                @pl.when((s >= lo) & (s < hi))
                def _(plan=PLAN[lo]):
                    action(plan)

                lo = hi

    def send(s, plan, *ks, part=None):
        for k in ks:
            message(s, k, False, plan, part).start()

    def arrive(s, plan, *ks, part=None):
        for k in ks:
            message(s, k, True, plan, part).wait_recv()

    def stage_a(s):
        for h in range(2):
            own_copy(s, h).wait()
        send(s, PLAN[0], 0, 1, 2)

    def stage_b(s, part=None, first=True):
        def steps(plan):
            if first:
                arrive(s, plan, 2)
            send(s, plan, 3, 4, part=part)
            if first:
                arrive(s, plan, 0)
            send(s, plan, 5, 7, part=part)
            if first:
                arrive(s, plan, 1)
            send(s, plan, 6, 8, part=part)

        by_plan(s, steps)

    def stage_c(s, part=None):
        def steps(plan):
            arrive(s, plan, 3, part=part)
            send(s, plan, 9, part=part)
            arrive(s, plan, 4, part=part)
            send(s, plan, 10, part=part)
            arrive(s, plan, 6, part=part)
            send(s, plan, 11, part=part)

        by_plan(s, steps)

    def gathered(s, part=None):
        by_plan(s, lambda plan: arrive(s, plan, 5, 7, 8, 9, 10, 11, part=part))

    def core_copy(s, part=None):
        src = prod.at[s, 1 - c] if part is None else prod.at[s, part]
        return pltpu.make_async_remote_copy(
            src_ref=src, dst_ref=cr.at[s], send_sem=ds_.at[s], recv_sem=dr.at[s],
            device_id=sibling, device_id_type=MESH,
        )

    def x_copy(s):
        dx = offset(s, c)
        slot = (1 - s // 4) * 3 + (dx + 3) % 4
        return pltpu.make_async_remote_copy(
            src_ref=prod.at[s, c], dst_ref=xr.at[slot], send_sem=xs_.at[s], recv_sem=xr_.at[slot],
            device_id=device((x + dx) % 4, yh, c, z, yl), device_id_type=MESH,
        )

    def x_arrive(slot):
        pltpu.make_async_remote_copy(
            src_ref=xr.at[slot], dst_ref=xr.at[slot], send_sem=xs_.at[0], recv_sem=xr_.at[slot],
            device_id=sibling, device_id_type=MESH,
        ).wait_recv()

    y_copy = pltpu.make_async_remote_copy(
        src_ref=ys, dst_ref=yr, send_sem=ysem.at[0], recv_sem=ysem.at[1],
        device_id=device(x, 1 - yh, c, z, yl), device_id_type=MESH,
    )

    group1 = [
        ((x + dx) % 4, (c + dc) % 2, (dx * 2 + dc)) for dx in range(4) for dc in range(2) if dx or dc
    ]
    y = yh * 2 + yl
    group2 = [
        ((y + dy) % 4, (z + dz) % 4, (dy * 4 + dz)) for dy in range(4) for dz in range(4) if dy or dz
    ]

    def one_copy(px, pc, slot):
        return pltpu.make_async_remote_copy(
            src_ref=one.at[0], dst_ref=one.at[slot], send_sem=s1.at[slot], recv_sem=r1.at[slot],
            device_id=device(px, yh, pc, z, yl), device_id_type=MESH,
        )

    def two_copy(py, pz, slot):
        return pltpu.make_async_remote_copy(
            src_ref=two.at[0], dst_ref=two.at[slot], send_sem=s2.at[slot], recv_sem=r2.at[slot],
            device_id=device(x, py // 2, c, pz, py % 2), device_id_type=MESH,
        )

    for s in range(PARTS):
        for h in range(2):
            own_copy(s, h).start()
        if s == 0:
            ctx_copy.start()
    for s in range(PARTS):
        for h in range(2):
            w_copy(s, h).start()
    first_copy.start()
    second_copy.start()

    barrier = pltpu.get_barrier_semaphore()
    for px, pc, _ in group1:
        pl.semaphore_signal(barrier, inc=1, device_id=device(px, yh, pc, z, yl), device_id_type=MESH)
    for py, pz, _ in group2:
        pl.semaphore_signal(barrier, inc=1, device_id=device(x, py // 2, c, pz, py % 2), device_id_type=MESH)
    pl.semaphore_wait(barrier, len(group1) + len(group2))

    stage_a(0)
    ctx_copy.wait()
    for k in range(cx.shape[0] // 128):
        cxt[:, k * 128 : (k + 1) * 128] = cx[k * 128 : (k + 1) * 128, :].T

    def product(s, lo, hi):
        for start in range(lo, hi, 256):
            width = min(256, hi - start)
            value = jnp.dot(cxt[...], gath[s, :, start : start + width], preferred_element_type=F32)
            value = (value * multiplier).astype(BF16)
            for k in range(0, width, 128):
                column = start + k
                prod[s, column // half, :, column % half : column % half + 128] = value[:, k : k + 128]

    def context_part(s, final):
        if not final:
            for h in range(2):
                w_copy(s, h).wait()

        @pl.loop(0, acc.shape[1] // 256)
        def _(n):
            cols = pl.ds(pl.multiple_of(n * 256, 256), 256)
            value = jnp.dot(gath[s], wv[s, :, cols], preferred_element_type=F32)
            if final:
                cg[:, cols] = ((acc[:, cols] + value) * multiplier).astype(BF16)
            else:
                acc[:, cols] += value

    def whole(s):
        gathered(s)
        product(s, 0, 2 * half)
        core_copy(s).start()

    def cores_sum(s):
        core_copy(s).wait_recv()

        @pl.when(s % 4 != 3)
        def _():
            prod[s, c] = (prod[s, c].astype(F32) + cr[s].astype(F32)).astype(BF16)
            x_copy(s).start()

    acc[...] = jnp.zeros_like(acc)

    @pl.loop(0, last)
    def _(i):
        @pl.when(i < last - 1)
        def _():
            stage_a(i + 1)

        stage_b(i)

        @pl.when(i > 0)
        def _():
            stage_c(i - 1)

        @pl.when(i == last - 1)
        def _():
            stage_a(last)

        @pl.when(i > 1)
        def _():
            s = i - 2
            whole(s)
            context_part(s, False)
            cores_sum(s)

            @pl.when(s == 3)
            def _():
                total = prod[3, c].astype(F32) + cr[3].astype(F32)
                for slot in range(3, 6):
                    x_arrive(slot)
                    total += xr[slot].astype(F32)
                ys[...] = total.astype(BF16)
                y_copy.start()

    whole(last - 2)
    stage_c(last - 1)
    cores_sum(last - 2)
    stage_b(last, part=0)
    stage_b(last, part=1, first=False)
    whole(last - 1)
    cores_sum(last - 1)
    stage_c(last, part=0)
    stage_c(last, part=1)
    gathered(last, part=0)
    product(last, 0, half)
    core_copy(last, 0).start()
    gathered(last, part=1)
    for start, width in ((0, 256), (256, 128)):
        value = jnp.dot(cxt[...], gath[last, :, half + start : half + start + width], preferred_element_type=F32)
        mine[:, start : start + width] = value * multiplier
    context_part(last - 2, False)
    first_copy.wait()
    second_copy.wait()
    for h in range(2):
        w_copy(last, h).wait()

    def fold(value):
        total = value[0:8, 0:128]
        for r in range(value.shape[0] // 8):
            for k in range(value.shape[1] // 128):
                if r or k:
                    total += value[r * 8 : (r + 1) * 8, k * 128 : (k + 1) * 128]
        return total[0:4] + total[4:8]

    w_sum = jnp.zeros((4, 128), F32)
    for k in range(half // 128):
        cols = slice(k * 128, (k + 1) * 128)
        w = wv[last, half + k * 128 : half + (k + 1) * 128, :].astype(F32)
        w_sum += fold(w * w)
        up[cols, :] = 0.1 * w
        mo[cols, :] = 0.9 * mo[cols, :]
        va[cols, :] = 0.95 * va[cols, :]
    y_copy.wait_recv()
    for slot in range(3):
        x_arrive(slot)
    core_copy(last, 0).wait_recv()
    for k in range(half // 128):
        cols = slice(k * 128, (k + 1) * 128)
        total = yr[:, cols].astype(F32) + cr[last, :, cols].astype(F32)
        for slot in range(3):
            total += xr[slot, :, cols].astype(F32)
        mine[:, cols] += total
    u_sum = jnp.zeros((4, 128), F32)
    for k in range(half // 128):
        cols = slice(k * 128, (k + 1) * 128)
        g = mine[:, cols].T
        m = mo[cols, :] + 0.1 * g
        v = va[cols, :] + 0.05 * g * g
        u = m / (jnp.sqrt(v) + 1e-06) + up[cols, :]
        mo[cols, :] = m
        va[cols, :] = v
        up[cols, :] = u
        u_sum += fold(u * u)
    one[0, 0:4] = u_sum
    one[0, 4:8] = w_sum
    for px, pc, slot in group1:
        one_copy(px, pc, slot).start()
    context_part(last - 1, False)
    for px, pc, slot in group1:
        one_copy(px, pc, slot).wait_recv()
    total = one[0]
    for _, _, slot in group1:
        total += one[slot]
    two[0] = total
    for py, pz, slot in group2:
        two_copy(py, pz, slot).start()
    context_part(last, True)

    @pl.loop(0, PARTS)
    def _(s):
        for k in range(3):
            message(s, k, False, PLAN[0]).wait_send()

        @pl.when(s < last)
        def _():
            def steps(plan):
                for k in range(3, len(MESSAGES)):
                    message(s, k, False, plan).wait_send()

            by_plan(s, steps)
            core_copy(s).wait_send()

        @pl.when(s % 4 != 3)
        def _():
            x_copy(s).wait_send()

    for part in range(2):
        for k in range(3, len(MESSAGES)):
            message(last, k, False, PLAN[last], part).wait_send()
    core_copy(last, 0).wait_send()
    y_copy.wait_send()
    for px, pc, slot in group1:
        one_copy(px, pc, slot).wait_send()
    for py, pz, slot in group2:
        two_copy(py, pz, slot).wait_recv()
    total = two[0]
    for _, _, slot in group2:
        total += two[slot]
    sums[...] = total
    for py, pz, slot in group2:
        two_copy(py, pz, slot).wait_send()


def finish(cg, mo, va, up, sums, cg_out, mo_out, va_out, la_out, la, sem):
    copies = [
        pltpu.make_async_copy(src, dst, sem.at[k])
        for k, (src, dst) in enumerate(((cg, cg_out), (mo, mo_out), (va, va_out)))
    ]
    for copy in copies:
        copy.start()
    u_total = jnp.sum(sums[0:4, :], keepdims=True)
    w_total = jnp.sum(sums[4:8, :], keepdims=True)
    la[...] = up[...] * (jnp.sqrt(w_total) / jnp.sqrt(u_total + 1e-06))
    copies.append(pltpu.make_async_copy(la, la_out, sem.at[3]))
    copies[-1].start()
    for copy in copies:
        copy.wait()


def shards(context, cotangent, weight, first_moment, second_moment):
    multiplier = 1.0 / math.sqrt(HEADS * HD)
    tokens, inner = context.shape
    rows, model = cotangent.shape
    part = model // PARTS
    half = part // 2
    sem = pltpu.SemaphoreType.DMA
    n = len(MESSAGES)
    scratch = [
        pltpu.VMEM((PARTS, tokens, part), BF16),
        pltpu.VMEM((PARTS, part, inner), BF16),
        pltpu.VMEM((tokens, inner), BF16),
        pltpu.VMEM((inner, tokens), BF16),
        pltpu.VMEM((PARTS, 2, inner, half), BF16),
        pltpu.VMEM((PARTS, inner, half), BF16),
        pltpu.VMEM((6, inner, half), BF16),
        pltpu.VMEM((inner, half), BF16),
        pltpu.VMEM((inner, half), BF16),
        pltpu.VMEM((tokens, inner), F32),
        pltpu.VMEM((inner, half), F32),
        pltpu.VMEM((8, 8, 128), F32),
        pltpu.VMEM((16, 8, 128), F32),
        sem((PARTS, 2)),
        sem((PARTS, 2)),
        sem((3,)),
        sem((PARTS, n)),
        sem((PARTS, n)),
        sem((2, n)),
        sem((2, n)),
        sem((PARTS,)),
        sem((PARTS,)),
        sem((PARTS,)),
        sem((6,)),
        sem((2,)),
        sem((8,)),
        sem((8,)),
        sem((16,)),
        sem((16,)),
    ]
    vmem = pl.BlockSpec(memory_space=pltpu.VMEM)
    anywhere = pl.BlockSpec(memory_space=pl.ANY)
    state = pltpu.VMEM(first_moment.shape, F32)
    results = pl.pallas_call(
        functools.partial(kernel, multiplier),
        out_shape=(pltpu.VMEM(context.shape, BF16), state, state, state, pltpu.VMEM((8, 128), F32)),
        in_specs=[anywhere] * 5,
        out_specs=[vmem] * 5,
        scratch_shapes=scratch,
        compiler_params=pltpu.CompilerParams(
            collective_id=0, has_side_effects=True, vmem_limit_bytes=56 * 2**20
        ),
        cost_estimate=pl.CostEstimate(
            flops=4 * tokens * inner * model, bytes_accessed=40 * 2**20, transcendentals=0
        ),
        name="step",
    )(cotangent, context, weight, first_moment, second_moment)
    results = [pltpu.with_memory_space_constraint(r, pltpu.VMEM) for r in results]
    state = jax.ShapeDtypeStruct(first_moment.shape, F32)
    return pl.pallas_call(
        finish,
        out_shape=(jax.ShapeDtypeStruct(context.shape, BF16), state, state, state),
        in_specs=[vmem] * 5,
        out_specs=[anywhere] * 4,
        scratch_shapes=[pltpu.VMEM(first_moment.shape, F32), sem((4,))],
        compiler_params=pltpu.CompilerParams(vmem_limit_bytes=4 * 2**20),
        name="finish",
    )(*results)


def solution(mesh):
    in_specs = (
        P("dp", "tensor"),
        P(("dp", "tensor"), None),
        P(None, "tensor"),
        P("dp", "tensor"),
        P("dp", "tensor"),
    )
    out_specs = (P("dp", "tensor"), P("dp", "tensor"), P("dp", "tensor"), P("dp", "tensor"))
    return jax.shard_map(shards, mesh=mesh, in_specs=in_specs, out_specs=out_specs, check_vma=False)
```
